512 devices in a mesh: tm: 2 (over core), space: 256 (over z, y, x).
Axes of the slice: x: 4, y: 8, z: 8, core: 2. Of those that a mesh axis runs over, the one named last changes fastest.
Arguments:
- initial_state: float32 [256, 320, 128], P('space'), may hold values from -6 to 6
- volume_block: float32 [320, 320], replicated, may hold values from -0.15625 to 0.15625
- face_blocks: float32 [6, 320, 80], replicated, may hold values from -0.125 to 0.125
- coarse_rate: float32 [320, 320], replicated, may hold values from -0.3125 to 0.3125
Outputs:
- start_states: float32 [4, 256, 320, 128], P('tm', 'space')
- fine_ends: float32 [4, 256, 320, 128], P('tm', 'space')
The draws below stay inside these ranges and needn't reach their ends.
All inputs are finite; a program needn't handle non-finite values.
Results may differ from the reference program's by a relative error of at most 0.0001.
Values sent between devices are 32-bit elements; how exact they have to be, the bound alone decides.
No kernel may reach another device: no remote copies, remote signals or barrier semaphores. Data moves between devices by JAX's collectives and lax.ppermute only.
A program may use at most 64 MiB of HBM per device.

```python
import jax
import jax.numpy as jnp
from jax import lax

F = 5
ITERS = 2
EY = 16
EZ = 8
FP = 320
FACE = 80
EYZ = 128
NEX = 256
NT = 4


def levels(key, extent, cuts, smallest, high):
    factor_of = 1.0
    for axis_at, shards_of in cuts:
        heights = jax.random.uniform(jax.random.fold_in(jax.random.fold_in(key, 6), axis_at), (shards_of,), jnp.float32, smallest / len(cuts), high / len(cuts))
        factor_of = factor_of * jnp.repeat(jnp.exp(heights), extent[axis_at] // shards_of).reshape((-1,) + (1,) * (len(extent) - 1 - axis_at))
    return factor_of


def scatter_about(stream_key, dims, deviation, most, pieces=(), dtype=jnp.bfloat16):
    array = jax.random.normal(stream_key, dims, jnp.float32) * deviation
    if len(pieces) > 0:
        array = levels(stream_key, dims, pieces, -0.22, 0.18) * array
    return jnp.clip(array, min=-most, max=most).astype(dtype)


def setup_inputs(seed: int = 0) -> dict:
    keys = jax.random.split(jax.random.key(seed), 5)
    return {
        "initial_state": scatter_about(keys[0], (NEX, FP, EYZ), 1.0, 6.0, ((0, 256),), jnp.float32),
        "volume_block": scatter_about(keys[1], (FP, FP), (4 * FP) ** -0.5, 0.15625, (), jnp.float32),
        "face_blocks": scatter_about(keys[2], (6, FP, FACE), (24 * FACE) ** -0.5, 0.125, (), jnp.float32),
        "coarse_rate": scatter_about(keys[3], (FP, FP), FP ** -0.5, 0.3125, (), jnp.float32),
    }


step_length = 0.25


def face(state, which, level):
    lead = state.shape[:-2]
    grid = state.reshape(lead + (F, 4, 4, 4, EY, EZ))
    picked = lax.index_in_dim(grid, level, len(lead) + 1 + which, keepdims=False)
    return picked.reshape(lead + (F * 16, EY, EZ))


def flatten(trace):
    return trace.reshape(trace.shape[:-2] + (EY * EZ,))


def apply(block, field):
    return jnp.einsum('ab,...bq->...aq', block, field, precision=lax.Precision.HIGHEST)


def assemble(state, volume_block, face_blocks, minus_x, plus_x):
    minus_y = flatten(jnp.roll(face(state, 1, 3), 1, axis=-2))
    plus_y = flatten(jnp.roll(face(state, 1, 0), -1, axis=-2))
    minus_z = flatten(jnp.roll(face(state, 2, 3), 1, axis=-1))
    plus_z = flatten(jnp.roll(face(state, 2, 0), -1, axis=-1))
    total = apply(volume_block, state) + apply(face_blocks[0], minus_x)
    total = total + apply(face_blocks[1], plus_x)
    total = total + apply(face_blocks[2], minus_y) + apply(face_blocks[3], plus_y)
    total = total + apply(face_blocks[4], minus_z) + apply(face_blocks[5], plus_z)
    return total


def evaluate(state, volume_block, face_blocks):
    upper = flatten(face(state, 0, 3))
    lower = flatten(face(state, 0, 0))
    minus_x = jnp.roll(upper, 1, axis=-3)
    plus_x = jnp.roll(lower, -1, axis=-3)
    return assemble(state, volume_block, face_blocks, minus_x, plus_x)


def reference(initial_state, volume_block, face_blocks, coarse_rate):
    def coarse(value):
        return value + step_length * apply(coarse_rate, value)

    def chain(corrections):
        starts = [initial_state]
        for slot in range(NT - 1):
            following = coarse(starts[-1])
            if corrections is not None:
                following = following + corrections[slot]
            starts.append(following)
        return starts

    starts = chain(None)
    middles = list(starts)
    lasts = list(starts)
    ends = []
    for turn in range(ITERS):
        ends = []
        corrections = []
        for slot in range(NT):
            start = starts[slot]
            fold = evaluate(jnp.stack([start, middles[slot], lasts[slot]]), volume_block, face_blocks)
            first = start + step_length * (5.0 / 24.0 * fold[0] + 1.0 / 3.0 * fold[1] - 1.0 / 24.0 * fold[2])
            second = first + 0.5 * step_length * (evaluate(first, volume_block, face_blocks) - fold[1])
            second = second + step_length * (-1.0 / 24.0 * fold[0] + 1.0 / 3.0 * fold[1] + 5.0 / 24.0 * fold[2])
            middles[slot] = first
            lasts[slot] = second
            ends.append(second)
            corrections.append(second - coarse(start))
        starts = chain(corrections)
    return jnp.stack(starts), jnp.stack(ends)
```

```python
import functools

import jax
import jax.numpy as jnp
from jax import lax
from jax.experimental import pallas as pl
from jax.experimental.pallas import tpu as pltpu
from jax.sharding import PartitionSpec as P

F = 5
EZ = 8
FP = 320
FACE = 80
EYZ = 128
NT = 4
ROW = 4
HALO = 4
WIN = 2 * HALO + 1
KR = FP + 6 * FACE
BF = jnp.bfloat16
F32 = jnp.float32


def split(value):
    high = value.astype(BF)
    low = (value - high.astype(F32)).astype(BF)
    return high, low


def x_rows(piece, level):
    return jnp.concatenate(
        [piece[f * 64 + 16 * level : f * 64 + 16 * level + 16] for f in range(F)], axis=0
    )


def y_face(value, level):
    wide = value.reshape(10, 32, EYZ)
    half = 8 * (level // 2)
    first, second = wide[:, half : half + 8], wide[:, 16 + half : 24 + half]
    upper_half = lax.broadcasted_iota(jnp.int32, (10, 8, EYZ), 1) >= 4
    if level % 2 == 1:
        first = pltpu.roll(first, 4, 1)
    else:
        second = pltpu.roll(second, 4, 1)
    return jnp.where(upper_half, second, first).reshape(FACE, EYZ)


def kernel(
    where,
    own,
    far,
    near,
    op_r,
    op_c,
    starts,
    ends,
    y,
    u1,
    u2,
    yp,
    w,
    v1,
    b,
    bc,
    up_op,
    lo_op,
):
    core, col, odd_row = where[0], where[1], where[2]

    y[HALO, 0] = own[...]
    y[2 * HALO, 0] = far[odd_row]
    y[0, 0] = far[1 - odd_row]

    def place(mate, own_block, other_block):
        y[mate - col + HALO, 0] = own_block
        y[jnp.where(mate > col, mate - col, mate - col + WIN - 1), 0] = other_block

    place(col + 1 - 2 * lax.rem(col, 2), near[0, 0:FP], near[0, FP : 2 * FP])
    place(ROW - 1 - col, near[1, 0:FP], near[1, FP : 2 * FP])
    place(lax.rem(col + 2, ROW), near[0, 2 * FP : 3 * FP], near[1, 2 * FP : 3 * FP])

    for f in range(F):
        up_op[16 * f : 16 * f + 16] = op_r[64 * f + 48 : 64 * f + 64]
        lo_op[16 * f : 16 * f + 16] = op_r[64 * f : 64 * f + 16]

    lane = lax.broadcasted_iota(jnp.int32, (FACE, EYZ), 1) % EZ

    def put(base, rows, lanes, value, size):
        high, low = split(value)
        b[base : base + rows, lanes] = high
        b[KR + base : KR + base + rows, lanes] = high
        b[2 * KR + base : 2 * KR + base + rows, lanes] = low

    def gather(state, at, minus_x, plus_x):
        for s in range(NT):
            lanes = slice(EYZ * s, EYZ * (s + 1))
            value = state[at, s]
            put(0, FP, lanes, value, FP)
            put(FP, FACE, lanes, minus_x(s), FACE)
            put(FP + FACE, FACE, lanes, plus_x(s), FACE)
            put(FP + 2 * FACE, FACE, lanes, pltpu.roll(y_face(value, 3), EZ, 1), FACE)
            put(FP + 3 * FACE, FACE, lanes, pltpu.roll(y_face(value, 0), EYZ - EZ, 1), FACE)
            low_z = state[at, s, pl.ds(3, FACE, stride=4), :]
            high_z = state[at, s, pl.ds(0, FACE, stride=4), :]
            put(
                FP + 4 * FACE,
                FACE,
                lanes,
                jnp.where(lane == 0, pltpu.roll(low_z, EYZ - EZ + 1, 1), pltpu.roll(low_z, 1, 1)),
                FACE,
            )
            put(
                FP + 5 * FACE,
                FACE,
                lanes,
                jnp.where(
                    lane == EZ - 1, pltpu.roll(high_z, EZ - 1, 1), pltpu.roll(high_z, EYZ - 1, 1)
                ),
                FACE,
            )

    def x_face(state, at, level):
        return lambda s: x_rows(state[at, s], level)

    def dot(left, right):
        return jnp.dot(left, right, preferred_element_type=F32)

    def lanes_of(product, s):
        return product[:, EYZ * s : EYZ * (s + 1)]

    def coarse(values):
        for k, value in enumerate(values):
            lanes = slice(EYZ * k, EYZ * (k + 1))
            high, low = split(value)
            bc[0:FP, lanes] = high
            bc[FP : 2 * FP, lanes] = high
            bc[2 * FP : 3 * FP, lanes] = low
        product = dot(op_c[...], bc[:, : EYZ * len(values)])
        return [value + lanes_of(product, k) for k, value in enumerate(values)]

    for n in range(NT - 1):
        for k, value in enumerate(coarse([y[k, n] for k in range(WIN)])):
            y[k, n + 1] = value

    def first_node(k, carry):
        gather(y, k + 1, x_face(y, k, 3), x_face(y, k + 2, 0))
        product = dot(op_r[...], b[...])
        for s in range(NT):
            u1[k, s] = y[k + 1, s] + lanes_of(product, s)
        return carry

    lax.fori_loop(0, 7, first_node, 0)

    def second_node(k, carry):
        gather(u1, k + 1, x_face(u1, k, 3), x_face(u1, k + 2, 0))
        product = dot(op_r[...], b[...])
        for s in range(NT):
            u2[k, s] = u1[k + 1, s] + lanes_of(product, s)
        return carry

    lax.fori_loop(0, 5, second_node, 0)

    for k in range(5):
        yp[k, 0] = y[k + 2, 0]
        yp[k, 1] = u2[k, 0]
    for n in (1, 2):
        change = coarse([yp[k, n] - y[k + 2, n] for k in range(5)])
        for k in range(5):
            yp[k, n + 1] = u2[k, n] + change[k]

    for k in range(5):
        for s in range(NT):
            w[k, s] = (5.0 / 12.0) * yp[k, s] + (2.0 / 3.0) * u1[k + 1, s] - (1.0 / 12.0) * u2[k, s]

    gather(w, 2, x_face(w, 1, 3), x_face(w, 3, 0))
    product = dot(op_r[...], b[...])
    for s in range(NT):
        v1[s] = (1.0 / 3.0) * (yp[2, s] + u1[3, s] + u2[2, s]) + (
            yp[2, s] + lanes_of(product, s)
        )

    sides = []
    for at, level, op in ((1, 3, up_op), (3, 0, lo_op)):
        gather(w, at, x_face(w, at - 1, 3), x_face(w, at + 1, 0))
        product = dot(op[...], b[...])
        side = []
        for s in range(NT):
            start = x_rows(yp[at, s], level)
            side.append(
                (1.0 / 3.0) * (start + x_rows(u1[at + 1, s], level) + x_rows(u2[at, s], level))
                + (start + lanes_of(product, s))
            )
        sides.append(side)
    for s in range(NT):
        w[2, s] = v1[s]
    gather(w, 2, lambda s: sides[0][s], lambda s: sides[1][s])
    product = dot(op_r[...], b[...])
    last = [yp[2, s] + lanes_of(product, s) for s in range(NT)]

    begin = [own[...], last[0]]
    for n in (1, 2):
        begin.append(last[n] + coarse([begin[n] - yp[2, n]])[0])

    @pl.when(core == 0)
    def _():
        for k in range(2):
            starts[k] = begin[k]
            ends[k] = last[k]

    @pl.when(core == 1)
    def _():
        for k in range(2):
            starts[k] = begin[2 + k]
            ends[k] = last[2 + k]


def work(where, own, far, near, op_r, op_c):
    vmem = pl.BlockSpec(memory_space=pltpu.VMEM)
    out = jax.ShapeDtypeStruct((2, FP, EYZ), F32)
    return pl.pallas_call(
        kernel,
        out_shape=(out, out),
        in_specs=[pl.BlockSpec(memory_space=pltpu.SMEM)] + [vmem] * 5,
        out_specs=(vmem, vmem),
        scratch_shapes=[
            pltpu.VMEM((WIN, NT, FP, EYZ), F32),
            pltpu.VMEM((7, NT, FP, EYZ), F32),
            pltpu.VMEM((5, NT, FP, EYZ), F32),
            pltpu.VMEM((5, NT, FP, EYZ), F32),
            pltpu.VMEM((5, NT, FP, EYZ), F32),
            pltpu.VMEM((NT, FP, EYZ), F32),
            pltpu.VMEM((3 * KR, NT * EYZ), BF),
            pltpu.VMEM((3 * FP, WIN * EYZ), BF),
            pltpu.VMEM((FACE, 3 * KR), BF),
            pltpu.VMEM((FACE, 3 * KR), BF),
        ],
        compiler_params=pltpu.CompilerParams(vmem_limit_bytes=48 << 20),
        name="parareal",
    )(where, own, far, near, op_r, op_c)


def operator(block):
    high = lax.reduce_precision(block, 8, 7)
    low = block - high
    return jnp.concatenate([high, low, high], axis=1).astype(BF)


def pairs(mate_of, spaces):
    groups = []
    for core in range(2):
        for place in range(spaces):
            mate = mate_of(core, place)
            assert mate_of(core, mate) == place
            if place < mate:
                groups.append([core * spaces + place, core * spaces + mate])
    return groups


def swapped(block, mate_of, spaces):
    both = lax.all_gather(block, ("tm", "space"), axis_index_groups=pairs(mate_of, spaces))
    core, place = lax.axis_index("tm"), lax.axis_index("space")
    mate = mate_of(core, place)
    return jnp.where(mate > place, both[1], both[0])


def other_row(spaces):
    def mate_of(core, place):
        down = (place // ROW + core) % 2
        return (place + ROW - 2 * ROW * down + spaces) % spaces

    return mate_of


def row_near(core, place):
    base, col = place // ROW * ROW, place % ROW
    return base + (1 - core) * (col + 1 - 2 * (col % 2)) + core * (ROW - 1 - col)


def row_far(core, place):
    return place // ROW * ROW + (place % ROW + 2) % ROW


def per_device(initial_state, volume_block, face_blocks, coarse_rate):
    spaces = lax.axis_size("space")
    core, place = lax.axis_index("tm"), lax.axis_index("space")
    col, odd_row = place % ROW, place // ROW % 2
    own = initial_state[0]

    across = swapped(own, other_row(spaces), spaces)
    far = lax.all_gather(across, "tm")
    above, below = far[odd_row], far[1 - odd_row]

    gives_above = jnp.where(core == 0, col % 2 == 0, col < 2)
    close = swapped(
        jnp.concatenate([own, jnp.where(gives_above, above, below)], axis=0), row_near, spaces
    )
    distant = swapped(
        jnp.where(core == 0, own, jnp.where(col < 2, above, below)), row_far, spaces
    )
    near = lax.all_gather(jnp.concatenate([close, distant], axis=0), "tm")

    step = 0.25
    blocks = jnp.concatenate([volume_block] + [face_blocks[k] for k in range(6)], axis=1)
    op_r = operator(0.5 * step * blocks)
    op_c = operator(step * coarse_rate)
    where = jnp.stack([core, col, odd_row]).astype(jnp.int32)
    starts, ends = work(where, own, far, near, op_r, op_c)
    return starts[:, None], ends[:, None]


def solution(mesh):
    return jax.shard_map(
        per_device,
        mesh=mesh,
        in_specs=(P("space", None, None), P(), P(), P()),
        out_specs=(P("tm", "space", None, None), P("tm", "space", None, None)),
        check_vma=False,
    )
```

```python
import functools

import jax
import jax.numpy as jnp
from jax import lax
from jax.experimental import pallas as pl
from jax.experimental.pallas import tpu as pltpu
from jax.sharding import PartitionSpec as P

F = 5
EZ = 8
FP = 320
FACE = 80
EYZ = 128
NT = 4
ROW = 4
HALO = 4
WIN = 2 * HALO + 1
KR = FP + 6 * FACE
MAIN = 768
REST = KR - MAIN
CMAIN = 256
CREST = FP - CMAIN
BF = jnp.bfloat16
F32 = jnp.float32


def split(value):
    high = value.astype(BF)
    low = (value - high.astype(F32)).astype(BF)
    return high, low


def dot(left, right):
    return jnp.dot(left, right, preferred_element_type=F32)


def dot_first(left, right):
    return lax.dot_general(left, right, (((0,), (0,)), ((), ())), preferred_element_type=F32)


def x_rows(piece, level):
    return jnp.concatenate(
        [piece[f * 64 + 16 * level : f * 64 + 16 * level + 16] for f in range(F)], axis=0
    )


def y_face(value, level):
    wide = value.reshape(10, 32, EYZ)
    half = 8 * (level // 2)
    first, second = wide[:, half : half + 8], wide[:, 16 + half : 24 + half]
    upper_half = lax.broadcasted_iota(jnp.int32, (10, 8, EYZ), 1) >= 4
    if level % 2 == 1:
        first = pltpu.roll(first, 4, 1)
    else:
        second = pltpu.roll(second, 4, 1)
    return jnp.where(upper_half, second, first).reshape(FACE, EYZ)


def lanes_of(product, s):
    return product[:, EYZ * s : EYZ * (s + 1)]


def side_by_side(ref, high, low, main, rest):
    for k, part in enumerate((high, low, high)):
        ref[:, main * k : main * (k + 1)] = part[:, :main]
        ref[:, 3 * main + rest * k : 3 * main + rest * (k + 1)] = part[:, main:]


def coarse(op_c, bc, values):
    for k, value in enumerate(values):
        lanes = slice(EYZ * k, EYZ * (k + 1))
        high, low = split(value)
        for j, part in enumerate((high, high, low)):
            bc[CMAIN * j : CMAIN * (j + 1), lanes] = part[:CMAIN]
            bc[3 * CMAIN + CREST * j : 3 * CMAIN + CREST * (j + 1), lanes] = part[CMAIN:]
    product = dot(op_c[...], bc[:, : EYZ * len(values)])
    return [value + lanes_of(product, k) for k, value in enumerate(values)]


def prepare(own, far, volume, faces, rate, op_r, op_c, y, bc):
    step = 0.25
    side_by_side(op_c, *split(step * rate[...]), CMAIN, CREST)
    for k, start in enumerate((own[...], far[0], far[1])):
        y[k, 0] = start
    for n in range(NT - 1):
        for k, value in enumerate(coarse(op_c, bc, [y[k, n] for k in range(3)])):
            y[k, n + 1] = value

    def placed(rows, first):
        at = lax.broadcasted_iota(jnp.int32, (rows, KR), 0) + first
        return jnp.where(at == lax.broadcasted_iota(jnp.int32, (rows, KR), 1), 1.0, 0.0).astype(BF)

    here, there = placed(FP, 0), placed(6 * FACE, FP)
    volumes = split(0.5 * step * volume[...])
    fluxes = split(0.5 * step * faces[...])
    high, low = [
        (dot(v, here) + dot_first(f, there)).astype(BF) for v, f in zip(volumes, fluxes)
    ]
    side_by_side(op_r, high, low, MAIN, REST)


def sweeps(where, ready, near, op_r, op_c, starts, ends, y, u1, u2, yp, w, b0, b1, bc, up_op, lo_op):
    core, col, odd_row = where[0], where[1], where[2]

    def place(mate, own_block, other_block):
        y[mate - col + HALO, 0] = own_block
        y[jnp.where(mate > col, mate - col, mate - col + WIN - 1), 0] = other_block

    place(col + 1 - 2 * lax.rem(col, 2), near[0, 0:FP], near[0, FP : 2 * FP])
    place(ROW - 1 - col, near[1, 0:FP], near[1, FP : 2 * FP])
    place(lax.rem(col + 2, ROW), near[0, 2 * FP : 3 * FP], near[1, 2 * FP : 3 * FP])
    for s in range(NT):
        y[HALO, s] = ready[0, s]
        y[2 * HALO, s] = ready[1 + odd_row, s]
        y[0, s] = ready[2 - odd_row, s]

    for f in range(F):
        up_op[16 * f : 16 * f + 16] = op_r[64 * f + 48 : 64 * f + 64]
        lo_op[16 * f : 16 * f + 16] = op_r[64 * f : 64 * f + 16]

    lane = lax.broadcasted_iota(jnp.int32, (FACE, EYZ), 1) % EZ

    def put(b, base, lanes, value):
        rows = value.shape[0]
        whole = min(rows, MAIN - base)
        high, low = split(value)
        for k, part in enumerate((high, high, low)):
            b[MAIN * k + base : MAIN * k + base + whole, lanes] = part[:whole]
            if whole < rows:
                b[3 * MAIN + REST * k : 3 * MAIN + REST * (k + 1), lanes] = part[whole:]

    def gather(b, state, at, minus_x, plus_x, slices=range(NT)):
        for s in slices:
            lanes = slice(EYZ * s, EYZ * (s + 1))
            value = state[at, s]
            put(b, 0, lanes, value)
            put(b, FP, lanes, minus_x(s))
            put(b, FP + FACE, lanes, plus_x(s))
            put(b, FP + 2 * FACE, lanes, pltpu.roll(y_face(value, 3), EZ, 1))
            put(b, FP + 3 * FACE, lanes, pltpu.roll(y_face(value, 0), EYZ - EZ, 1))
            low_z = state[at, s, pl.ds(3, FACE, stride=4), :]
            high_z = state[at, s, pl.ds(0, FACE, stride=4), :]
            low_z = jnp.where(
                lane == 0, pltpu.roll(low_z, EYZ - EZ + 1, 1), pltpu.roll(low_z, 1, 1)
            )
            high_z = jnp.where(
                lane == EZ - 1, pltpu.roll(high_z, EZ - 1, 1), pltpu.roll(high_z, EYZ - 1, 1)
            )
            put(b, FP + 4 * FACE, lanes, low_z)
            put(b, FP + 5 * FACE, lanes, high_z)

    def x_face(state, at, level):
        return lambda s: x_rows(state[at, s], level)

    def x_store(state, at, s, level, rows):
        for f in range(F):
            state[at, s, 64 * f + 16 * level : 64 * f + 16 * level + 16] = rows[
                16 * f : 16 * f + 16
            ]

    here = (1, 2, 3, 5, 6, 7)
    for n in range(NT - 1):
        for k, value in zip(here, coarse(op_c, bc, [y[k, n] for k in here])):
            y[k, n + 1] = value

    def node(target, source, k, level=None, slices=None):
        slices = range(NT) if slices is None else slices
        low, high = EYZ * slices[0], EYZ * (slices[-1] + 1)

        def load(b):
            gather(b, source, k + 1, x_face(source, k, 3), x_face(source, k + 2, 0), slices)

        def run(b):
            if level is None:
                product = dot(op_r[...], b[:, low:high])
            else:
                product = dot((lo_op if level == 0 else up_op)[...], b[:, low:high])
            for j, s in enumerate(slices):
                if level is None:
                    target[k, s] = source[k + 1, s] + lanes_of(product, j)
                else:
                    x_store(
                        target, k, s, level, x_rows(source[k + 1, s], level) + lanes_of(product, j)
                    )

        return load, run

    def first(k):
        return node(u1, y, k, {0: 3, 6: 0}.get(k))

    def second(k, *rest):
        return node(u2, u1, k, *rest)

    tasks = [
        first(0),
        first(1),
        first(2),
        first(3),
        second(0, None, range(2)),
        second(0, 3, range(2, 4)),
        first(4),
        second(1),
        first(5),
        second(2),
        first(6),
        second(3),
        second(4, None, range(2)),
        second(4, 0, range(2, 4)),
    ]
    buffers = (b0, b1)
    tasks[0][0](b0)
    for i, (_, run) in enumerate(tasks):
        if i + 1 < len(tasks):
            tasks[i + 1][0](buffers[(i + 1) % 2])
        run(buffers[i % 2])

    for k in range(5):
        yp[k, 0] = y[k + 2, 0]
        yp[k, 1] = u2[k, 0]
    for n in (1, 2):
        change = coarse(op_c, bc, [yp[k, n] - y[k + 2, n] for k in range(5)])
        for k in range(5):
            if n == 2 and k in (0, 4):
                level = 3 if k == 0 else 0
                x_store(
                    yp, k, n + 1, level, x_rows(u2[k, n], level) + x_rows(change[k], level)
                )
            else:
                yp[k, n + 1] = u2[k, n] + change[k]

    for k in range(1, 4):
        for s in range(NT):
            w[k, s] = (5.0 / 12.0) * yp[k, s] + (2.0 / 3.0) * u1[k + 1, s] - (1.0 / 12.0) * u2[k, s]
    for k, level in ((0, 3), (4, 0)):
        for s in range(NT):
            x_store(
                w,
                k,
                s,
                level,
                (5.0 / 12.0) * x_rows(yp[k, s], level)
                + (2.0 / 3.0) * x_rows(u1[k + 1, s], level)
                - (1.0 / 12.0) * x_rows(u2[k, s], level),
            )

    def combine(start, one, two, product):
        return (1.0 / 3.0) * (start + one + two) + (start + product)

    sides = []
    gather(b0, w, 1, x_face(w, 0, 3), x_face(w, 2, 0))
    gather(b1, w, 3, x_face(w, 2, 3), x_face(w, 4, 0))
    product = dot(up_op[...], b0[...])
    for at, level, b, op in ((1, 3, b0, up_op), (3, 0, b1, lo_op)):
        product = dot(op[...], b[...])
        sides.append(
            [
                combine(
                    x_rows(yp[at, s], level),
                    x_rows(u1[at + 1, s], level),
                    x_rows(u2[at, s], level),
                    lanes_of(product, s),
                )
                for s in range(NT)
            ]
        )
    gather(b0, w, 2, x_face(w, 1, 3), x_face(w, 3, 0))
    product = dot(op_r[...], b0[...])
    for s in range(NT):
        w[2, s] = combine(yp[2, s], u1[3, s], u2[2, s], lanes_of(product, s))
    gather(b1, w, 2, lambda s: sides[0][s], lambda s: sides[1][s])
    product = dot(op_r[...], b1[...])
    last = [yp[2, s] + lanes_of(product, s) for s in range(NT)]

    begin = [y[HALO, 0], last[0]]
    for n in (1, 2):
        begin.append(last[n] + coarse(op_c, bc, [begin[n] - yp[2, n]])[0])

    @pl.when(core == 0)
    def _():
        for k in range(2):
            starts[k] = begin[k]
            ends[k] = last[k]

    @pl.when(core == 1)
    def _():
        for k in range(2):
            starts[k] = begin[2 + k]
            ends[k] = last[2 + k]


VMEM = pl.BlockSpec(memory_space=pltpu.VMEM)
LIMIT = pltpu.CompilerParams(vmem_limit_bytes=48 << 20)


def ready_made(own, far, volume, faces, rate):
    return pl.pallas_call(
        prepare,
        out_shape=(
            jax.ShapeDtypeStruct((FP, 3 * KR), BF),
            jax.ShapeDtypeStruct((FP, 3 * FP), BF),
            jax.ShapeDtypeStruct((3, NT, FP, EYZ), F32),
        ),
        in_specs=[VMEM] * 5,
        out_specs=(VMEM,) * 3,
        scratch_shapes=[pltpu.VMEM((3 * FP, 3 * EYZ), BF)],
        compiler_params=pltpu.CompilerParams(vmem_limit_bytes=24 << 20),
        cost_estimate=pl.CostEstimate(
            flops=4 * 10**9, bytes_accessed=6 * 10**6, transcendentals=0
        ),
        name="prepare",
    )(own, far, volume, faces, rate)


def work(where, ready, near, op_r, op_c):
    out = jax.ShapeDtypeStruct((2, FP, EYZ), F32)
    return pl.pallas_call(
        sweeps,
        out_shape=(out, out),
        in_specs=[pl.BlockSpec(memory_space=pltpu.SMEM)] + [VMEM] * 4,
        out_specs=(VMEM, VMEM),
        scratch_shapes=[
            pltpu.VMEM((WIN, NT, FP, EYZ), F32),
            pltpu.VMEM((7, NT, FP, EYZ), F32),
            pltpu.VMEM((5, NT, FP, EYZ), F32),
            pltpu.VMEM((5, NT, FP, EYZ), F32),
            pltpu.VMEM((5, NT, FP, EYZ), F32),
            pltpu.VMEM((3 * KR, NT * EYZ), BF),
            pltpu.VMEM((3 * KR, NT * EYZ), BF),
            pltpu.VMEM((3 * FP, 6 * EYZ), BF),
            pltpu.VMEM((FACE, 3 * KR), BF),
            pltpu.VMEM((FACE, 3 * KR), BF),
        ],
        compiler_params=LIMIT,
        name="sweeps",
    )(where, ready, near, op_r, op_c)


def pairs(mate_of, spaces):
    groups = []
    for core in range(2):
        for place in range(spaces):
            mate = mate_of(core, place)
            assert mate_of(core, mate) == place
            if place < mate:
                groups.append([core * spaces + place, core * spaces + mate])
    return groups


def swapped(block, mate_of, spaces):
    both = lax.all_gather(block, ("tm", "space"), axis_index_groups=pairs(mate_of, spaces))
    core, place = lax.axis_index("tm"), lax.axis_index("space")
    mate = mate_of(core, place)
    return jnp.where(mate > place, both[1], both[0])


def sent(block, mate_of, spaces):
    route = [route for a, b in pairs(mate_of, spaces) for route in ((a, b), (b, a))]
    return lax.ppermute(block, ("tm", "space"), route)


def other_row(spaces):
    def mate_of(core, place):
        down = (place // ROW + core) % 2
        return (place + ROW - 2 * ROW * down + spaces) % spaces

    return mate_of


def row_near(core, place):
    base, col = place // ROW * ROW, place % ROW
    return base + (1 - core) * (col + 1 - 2 * (col % 2)) + core * (ROW - 1 - col)


def row_far(core, place):
    return place // ROW * ROW + (place % ROW + 2) % ROW


def per_device(initial_state, volume_block, face_blocks, coarse_rate):
    spaces = lax.axis_size("space")
    core, place = lax.axis_index("tm"), lax.axis_index("space")
    col, odd_row = place % ROW, place // ROW % 2
    own = initial_state[0]

    across = swapped(own, other_row(spaces), spaces)
    far = lax.all_gather(across, "tm")
    above, below = far[odd_row], far[1 - odd_row]

    distant = sent(jnp.where(core == 0, own, jnp.where(col < 2, above, below)), row_far, spaces)
    gives_above = jnp.where(core == 0, col % 2 == 0, col < 2)
    close = sent(
        jnp.concatenate([own, jnp.where(gives_above, above, below)], axis=0), row_near, spaces
    )
    faces = jnp.transpose(face_blocks, (0, 2, 1)).reshape(6 * FACE, FP)
    op_r, op_c, ready = ready_made(own, far, volume_block, faces, coarse_rate)
    near = lax.all_gather(jnp.concatenate([close, distant], axis=0), "tm")

    where = jnp.stack([core, col, odd_row]).astype(jnp.int32)
    starts, ends = work(where, ready, near, op_r, op_c)
    return starts[:, None], ends[:, None]


def solution(mesh):
    return jax.shard_map(
        per_device,
        mesh=mesh,
        in_specs=(P("space", None, None), P(), P(), P()),
        out_specs=(P("tm", "space", None, None), P("tm", "space", None, None)),
        check_vma=False,
    )
```

```python
import functools

import jax
import jax.numpy as jnp
from jax import lax
from jax.experimental import pallas as pl
from jax.experimental.pallas import tpu as pltpu
from jax.sharding import PartitionSpec as P

F = 5
EZ = 8
FP = 320
FACE = 80
EYZ = 128
NT = 4
ROW = 4
HALO = 4
WIN = 2 * HALO + 1
KR = FP + 6 * FACE
MAIN = 768
REST = KR - MAIN
CMAIN = 256
CREST = FP - CMAIN
BF = jnp.bfloat16
F32 = jnp.float32


def split(value):
    high = value.astype(BF)
    low = (value - high.astype(F32)).astype(BF)
    return high, low


def dot(left, right):
    return jnp.dot(left, right, preferred_element_type=F32)


def dot_first(left, right):
    return lax.dot_general(left, right, (((0,), (0,)), ((), ())), preferred_element_type=F32)


def x_rows(piece, level):
    return jnp.concatenate(
        [piece[f * 64 + 16 * level : f * 64 + 16 * level + 16] for f in range(F)], axis=0
    )


def y_face(value, level):
    wide = value.reshape(10, 32, EYZ)
    half = 8 * (level // 2)
    first, second = wide[:, half : half + 8], wide[:, 16 + half : 24 + half]
    upper_half = lax.broadcasted_iota(jnp.int32, (10, 8, EYZ), 1) >= 4
    if level % 2 == 1:
        first = pltpu.roll(first, 4, 1)
    else:
        second = pltpu.roll(second, 4, 1)
    return jnp.where(upper_half, second, first).reshape(FACE, EYZ)


def lanes_of(product, s):
    return product[:, EYZ * s : EYZ * (s + 1)]


def side_by_side(ref, high, low, main, rest):
    for k, part in enumerate((high, low, high)):
        ref[:, main * k : main * (k + 1)] = part[:, :main]
        ref[:, 3 * main + rest * k : 3 * main + rest * (k + 1)] = part[:, main:]


def coarse(op_c, bc, values):
    for k, value in enumerate(values):
        lanes = slice(EYZ * k, EYZ * (k + 1))
        high, low = split(value)
        for j, part in enumerate((high, high, low)):
            bc[CMAIN * j : CMAIN * (j + 1), lanes] = part[:CMAIN]
            bc[3 * CMAIN + CREST * j : 3 * CMAIN + CREST * (j + 1), lanes] = part[CMAIN:]
    product = dot(op_c[...], bc[:, : EYZ * len(values)])
    return [value + lanes_of(product, k) for k, value in enumerate(values)]


def put(b, base, lanes, value):
    rows = value.shape[0]
    whole = min(rows, MAIN - base)
    high, low = split(value)
    for k, part in enumerate((high, high, low)):
        b[MAIN * k + base : MAIN * k + base + whole, lanes] = part[:whole]
        if whole < rows:
            b[3 * MAIN + REST * k : 3 * MAIN + REST * (k + 1), lanes] = part[whole:]


def gather(b, state, at, minus_x, plus_x, slices=range(NT)):
    lane = lax.broadcasted_iota(jnp.int32, (FACE, EYZ), 1) % EZ
    for s in slices:
        lanes = slice(EYZ * s, EYZ * (s + 1))
        value = state[at, s]
        put(b, 0, lanes, value)
        if minus_x is not None:
            put(b, FP, lanes, minus_x(s))
            put(b, FP + FACE, lanes, plus_x(s))
        put(b, FP + 2 * FACE, lanes, pltpu.roll(y_face(value, 3), EZ, 1))
        put(b, FP + 3 * FACE, lanes, pltpu.roll(y_face(value, 0), EYZ - EZ, 1))
        low_z = state[at, s, pl.ds(3, FACE, stride=4), :]
        high_z = state[at, s, pl.ds(0, FACE, stride=4), :]
        low_z = jnp.where(
            lane == 0, pltpu.roll(low_z, EYZ - EZ + 1, 1), pltpu.roll(low_z, 1, 1)
        )
        high_z = jnp.where(
            lane == EZ - 1, pltpu.roll(high_z, EZ - 1, 1), pltpu.roll(high_z, EYZ - 1, 1)
        )
        put(b, FP + 4 * FACE, lanes, low_z)
        put(b, FP + 5 * FACE, lanes, high_z)


def prepare(own, far, volume, faces, rate, op_r, op_x, op_c, y, part, bc, b):
    step = 0.25
    side_by_side(op_c, *split(step * rate[...]), CMAIN, CREST)
    for k, start in enumerate((own[...], far[0], far[1])):
        y[k, 0] = start
    for n in range(NT - 1):
        for k, value in enumerate(coarse(op_c, bc, [y[k, n] for k in range(3)])):
            y[k, n + 1] = value

    def placed(rows, first):
        at = lax.broadcasted_iota(jnp.int32, (rows, KR), 0) + first
        return jnp.where(at == lax.broadcasted_iota(jnp.int32, (rows, KR), 1), 1.0, 0.0).astype(BF)

    here, there = placed(FP, 0), placed(6 * FACE, FP)
    volumes = split(0.5 * step * volume[...])
    fluxes = split(0.5 * step * faces[...])
    high, low = [
        (dot(v, here) + dot_first(f, there)).astype(BF) for v, f in zip(volumes, fluxes)
    ]
    side_by_side(op_r, high, low, MAIN, REST)
    for k, columns in enumerate((high, low, high)):
        op_x[:, 2 * FACE * k : 2 * FACE * (k + 1)] = columns[:, FP : FP + 2 * FACE]

    gather(b, y, 0, None, None)
    for k in range(3):
        b[MAIN * k + FP : MAIN * k + FP + 2 * FACE] = jnp.zeros((2 * FACE, NT * EYZ), BF)
    product = dot(op_r[...], b[...])
    for s in range(NT):
        part[s] = y[0, s] + lanes_of(product, s)


def sweeps(ready, part, near, op_r, op_x, op_c, starts, ends, y, u1, u2, yp, w, b0, b1, bx, bc, up_op, lo_op):
    core, place_here = lax.axis_index("tm"), lax.axis_index("space")
    col, odd_row = lax.rem(place_here, ROW), lax.rem(lax.div(place_here, ROW), 2)

    def place(mate, own_block, other_block):
        y[mate - col + HALO, 0] = own_block
        y[jnp.where(mate > col, mate - col, mate - col + WIN - 1), 0] = other_block

    place(col + 1 - 2 * lax.rem(col, 2), near[0, 0:FP], near[0, FP : 2 * FP])
    place(ROW - 1 - col, near[1, 0:FP], near[1, FP : 2 * FP])
    place(lax.rem(col + 2, ROW), near[0, 2 * FP : 3 * FP], near[1, 2 * FP : 3 * FP])
    for s in range(NT):
        y[HALO, s] = ready[0, s]
        y[2 * HALO, s] = ready[1 + odd_row, s]
        y[0, s] = ready[2 - odd_row, s]

    for f in range(F):
        up_op[16 * f : 16 * f + 16] = op_r[64 * f + 48 : 64 * f + 64]
        lo_op[16 * f : 16 * f + 16] = op_r[64 * f : 64 * f + 16]

    def x_face(state, at, level):
        return lambda s: x_rows(state[at, s], level)

    def x_store(state, at, s, level, rows):
        for f in range(F):
            state[at, s, 64 * f + 16 * level : 64 * f + 16 * level + 16] = rows[
                16 * f : 16 * f + 16
            ]

    here = (1, 2, 3, 5, 6, 7)
    for n in range(NT - 1):
        for k, value in zip(here, coarse(op_c, bc, [y[k, n] for k in here])):
            y[k, n + 1] = value

    def node(target, source, k, level=None, slices=None):
        slices = range(NT) if slices is None else slices
        low, high = EYZ * slices[0], EYZ * (slices[-1] + 1)

        def load(b):
            gather(b, source, k + 1, x_face(source, k, 3), x_face(source, k + 2, 0), slices)

        def run(b):
            if level is None:
                product = dot(op_r[...], b[:, low:high])
            else:
                product = dot((lo_op if level == 0 else up_op)[...], b[:, low:high])
            for j, s in enumerate(slices):
                if level is None:
                    target[k, s] = source[k + 1, s] + lanes_of(product, j)
                else:
                    x_store(
                        target, k, s, level, x_rows(source[k + 1, s], level) + lanes_of(product, j)
                    )

        return load, run

    def first_here():
        def load(b):
            for s in range(NT):
                lanes = slice(EYZ * s, EYZ * (s + 1))
                for j, rows in enumerate((x_rows(y[HALO - 1, s], 3), x_rows(y[HALO + 1, s], 0))):
                    high, low = split(rows)
                    for k, piece in enumerate((high, high, low)):
                        at = 2 * FACE * k + FACE * j
                        bx[at : at + FACE, lanes] = piece

        def run(b):
            product = dot(op_x[...], bx[...])
            for s in range(NT):
                u1[3, s] = part[s] + lanes_of(product, s)

        return load, run

    def first(k):
        return node(u1, y, k, {0: 3, 6: 0}.get(k))

    def second(k, *rest):
        return node(u2, u1, k, *rest)

    tasks = [
        first(0),
        first(1),
        first(2),
        first_here(),
        second(0, None, range(2)),
        second(0, 3, range(2, 4)),
        first(4),
        second(1),
        first(5),
        second(2),
        first(6),
        second(3),
        second(4, None, range(2)),
        second(4, 0, range(2, 4)),
    ]
    buffers = (b0, b1)
    tasks[0][0](b0)
    for i, (_, run) in enumerate(tasks):
        if i + 1 < len(tasks):
            tasks[i + 1][0](buffers[(i + 1) % 2])
        run(buffers[i % 2])

    for k in range(5):
        yp[k, 0] = y[k + 2, 0]
        yp[k, 1] = u2[k, 0]
    for n in (1, 2):
        change = coarse(op_c, bc, [yp[k, n] - y[k + 2, n] for k in range(5)])
        for k in range(5):
            if n == 2 and k in (0, 4):
                level = 3 if k == 0 else 0
                x_store(
                    yp, k, n + 1, level, x_rows(u2[k, n], level) + x_rows(change[k], level)
                )
            else:
                yp[k, n + 1] = u2[k, n] + change[k]

    for k in range(1, 4):
        for s in range(NT):
            w[k, s] = (5.0 / 12.0) * yp[k, s] + (2.0 / 3.0) * u1[k + 1, s] - (1.0 / 12.0) * u2[k, s]
    for k, level in ((0, 3), (4, 0)):
        for s in range(NT):
            x_store(
                w,
                k,
                s,
                level,
                (5.0 / 12.0) * x_rows(yp[k, s], level)
                + (2.0 / 3.0) * x_rows(u1[k + 1, s], level)
                - (1.0 / 12.0) * x_rows(u2[k, s], level),
            )

    def combine(start, one, two, product):
        return (1.0 / 3.0) * (start + one + two) + (start + product)

    sides = []
    gather(b0, w, 1, x_face(w, 0, 3), x_face(w, 2, 0))
    gather(b1, w, 3, x_face(w, 2, 3), x_face(w, 4, 0))
    product = dot(up_op[...], b0[...])
    for at, level, b, op in ((1, 3, b0, up_op), (3, 0, b1, lo_op)):
        product = dot(op[...], b[...])
        sides.append(
            [
                combine(
                    x_rows(yp[at, s], level),
                    x_rows(u1[at + 1, s], level),
                    x_rows(u2[at, s], level),
                    lanes_of(product, s),
                )
                for s in range(NT)
            ]
        )
    gather(b0, w, 2, x_face(w, 1, 3), x_face(w, 3, 0))
    product = dot(op_r[...], b0[...])
    for s in range(NT):
        w[2, s] = combine(yp[2, s], u1[3, s], u2[2, s], lanes_of(product, s))
    gather(b1, w, 2, lambda s: sides[0][s], lambda s: sides[1][s])
    product = dot(op_r[...], b1[...])
    last = [yp[2, s] + lanes_of(product, s) for s in range(NT)]

    begin = [y[HALO, 0], last[0]]
    for n in (1, 2):
        begin.append(last[n] + coarse(op_c, bc, [begin[n] - yp[2, n]])[0])

    @pl.when(core == 0)
    def _():
        for k in range(2):
            starts[k] = begin[k]
            ends[k] = last[k]

    @pl.when(core == 1)
    def _():
        for k in range(2):
            starts[k] = begin[2 + k]
            ends[k] = last[2 + k]


VMEM = pl.BlockSpec(memory_space=pltpu.VMEM)
LIMIT = pltpu.CompilerParams(vmem_limit_bytes=48 << 20)


def ready_made(own, far, volume, faces, rate):
    return pl.pallas_call(
        prepare,
        out_shape=(
            jax.ShapeDtypeStruct((FP, 3 * KR), BF),
            jax.ShapeDtypeStruct((FP, 6 * FACE), BF),
            jax.ShapeDtypeStruct((FP, 3 * FP), BF),
            jax.ShapeDtypeStruct((3, NT, FP, EYZ), F32),
            jax.ShapeDtypeStruct((NT, FP, EYZ), F32),
        ),
        in_specs=[VMEM] * 5,
        out_specs=(VMEM,) * 5,
        scratch_shapes=[
            pltpu.VMEM((3 * FP, 3 * EYZ), BF),
            pltpu.VMEM((3 * KR, NT * EYZ), BF),
        ],
        compiler_params=pltpu.CompilerParams(vmem_limit_bytes=24 << 20),
        cost_estimate=pl.CostEstimate(
            flops=4 * 10**9, bytes_accessed=6 * 10**6, transcendentals=0
        ),
        name="prepare",
    )(own, far, volume, faces, rate)


def work(ready, part, near, op_r, op_x, op_c):
    out = jax.ShapeDtypeStruct((2, FP, EYZ), F32)
    return pl.pallas_call(
        sweeps,
        out_shape=(out, out),
        in_specs=[VMEM] * 6,
        out_specs=(VMEM, VMEM),
        scratch_shapes=[
            pltpu.VMEM((WIN, NT, FP, EYZ), F32),
            pltpu.VMEM((7, NT, FP, EYZ), F32),
            pltpu.VMEM((5, NT, FP, EYZ), F32),
            pltpu.VMEM((5, NT, FP, EYZ), F32),
            pltpu.VMEM((5, NT, FP, EYZ), F32),
            pltpu.VMEM((3 * KR, NT * EYZ), BF),
            pltpu.VMEM((3 * KR, NT * EYZ), BF),
            pltpu.VMEM((6 * FACE, NT * EYZ), BF),
            pltpu.VMEM((3 * FP, 6 * EYZ), BF),
            pltpu.VMEM((FACE, 3 * KR), BF),
            pltpu.VMEM((FACE, 3 * KR), BF),
        ],
        compiler_params=LIMIT,
        name="sweeps",
    )(ready, part, near, op_r, op_x, op_c)


def pairs(mate_of, spaces):
    groups = []
    for core in range(2):
        for place in range(spaces):
            mate = mate_of(core, place)
            assert mate_of(core, mate) == place
            if place < mate:
                groups.append([core * spaces + place, core * spaces + mate])
    return groups


def swapped(block, mate_of, spaces):
    both = lax.all_gather(block, ("tm", "space"), axis_index_groups=pairs(mate_of, spaces))
    core, place = lax.axis_index("tm"), lax.axis_index("space")
    first = mate_of(core, place) > place
    return jnp.where(first, both[1], both[0]), jnp.where(first, both[0], both[1])


def sent(block, mate_of, spaces):
    route = [route for a, b in pairs(mate_of, spaces) for route in ((a, b), (b, a))]
    return lax.ppermute(block, ("tm", "space"), route)


def other_row(spaces):
    def mate_of(core, place):
        down = (place // ROW + core) % 2
        return (place + ROW - 2 * ROW * down + spaces) % spaces

    return mate_of


def row_near(core, place):
    base, col = place // ROW * ROW, place % ROW
    return base + (1 - core) * (col + 1 - 2 * (col % 2)) + core * (ROW - 1 - col)


def row_far(core, place):
    return place // ROW * ROW + (place % ROW + 2) % ROW


def per_device(initial_state, volume_block, face_blocks, coarse_rate):
    spaces = lax.axis_size("space")
    core, place = lax.axis_index("tm"), lax.axis_index("space")
    col, odd_row = place % ROW, place // ROW % 2
    own = initial_state[0]

    across, own = swapped(own, other_row(spaces), spaces)
    far = lax.all_gather(across, "tm")
    above, below = far[odd_row], far[1 - odd_row]

    distant = sent(jnp.where(core == 0, own, jnp.where(col < 2, above, below)), row_far, spaces)
    gives_above = jnp.where(core == 0, col % 2 == 0, col < 2)
    close = sent(
        jnp.concatenate([own, jnp.where(gives_above, above, below)], axis=0), row_near, spaces
    )
    faces = jnp.transpose(face_blocks, (0, 2, 1)).reshape(6 * FACE, FP)
    op_r, op_x, op_c, ready, part = ready_made(own, far, volume_block, faces, coarse_rate)
    near = lax.all_gather(jnp.concatenate([close, distant], axis=0), "tm")

    starts, ends = work(ready, part, near, op_r, op_x, op_c)
    return starts[:, None], ends[:, None]


def solution(mesh):
    return jax.shard_map(
        per_device,
        mesh=mesh,
        in_specs=(P("space", None, None), P(), P(), P()),
        out_specs=(P("tm", "space", None, None), P("tm", "space", None, None)),
        check_vma=False,
    )
```

```python
import functools

import jax
import jax.numpy as jnp
from jax import lax
from jax.experimental import pallas as pl
from jax.experimental.pallas import tpu as pltpu
from jax.sharding import PartitionSpec as P

F = 5
EZ = 8
FP = 320
FACE = 80
EYZ = 128
NT = 4
ROW = 4
HALO = 4
WIN = 2 * HALO + 1
KR = FP + 6 * FACE
MAIN = 768
REST = KR - MAIN
CMAIN = 256
CREST = FP - CMAIN
BF = jnp.bfloat16
F32 = jnp.float32


def split(value):
    high = value.astype(BF)
    low = (value - high.astype(F32)).astype(BF)
    return high, low


def dot(left, right):
    return jnp.dot(left, right, preferred_element_type=F32)


def dot_first(left, right):
    return lax.dot_general(left, right, (((0,), (0,)), ((), ())), preferred_element_type=F32)


def x_rows(piece, level):
    return jnp.concatenate(
        [piece[f * 64 + 16 * level : f * 64 + 16 * level + 16] for f in range(F)], axis=0
    )


def y_face(value, level):
    wide = value.reshape(10, 32, EYZ)
    half = 8 * (level // 2)
    first, second = wide[:, half : half + 8], wide[:, 16 + half : 24 + half]
    upper_half = lax.broadcasted_iota(jnp.int32, (10, 8, EYZ), 1) >= 4
    if level % 2 == 1:
        first = pltpu.roll(first, 4, 1)
    else:
        second = pltpu.roll(second, 4, 1)
    return jnp.where(upper_half, second, first).reshape(FACE, EYZ)


def lanes_of(product, s):
    return product[:, EYZ * s : EYZ * (s + 1)]


def side_by_side(ref, high, low, main, rest):
    for k, part in enumerate((high, low, high)):
        ref[:, main * k : main * (k + 1)] = part[:, :main]
        ref[:, 3 * main + rest * k : 3 * main + rest * (k + 1)] = part[:, main:]


def coarse(op_c, bc, values):
    for k, value in enumerate(values):
        lanes = slice(EYZ * k, EYZ * (k + 1))
        high, low = split(value)
        for j, part in enumerate((high, high, low)):
            bc[CMAIN * j : CMAIN * (j + 1), lanes] = part[:CMAIN]
            bc[3 * CMAIN + CREST * j : 3 * CMAIN + CREST * (j + 1), lanes] = part[CMAIN:]
    product = dot(op_c[...], bc[:, : EYZ * len(values)])
    return [value + lanes_of(product, k) for k, value in enumerate(values)]


def put(b, base, lanes, value):
    rows = value.shape[0]
    whole = min(rows, MAIN - base)
    high, low = split(value)
    for k, part in enumerate((high, high, low)):
        b[MAIN * k + base : MAIN * k + base + whole, lanes] = part[:whole]
        if whole < rows:
            b[3 * MAIN + REST * k : 3 * MAIN + REST * (k + 1), lanes] = part[whole:]


def gather(b, state, at, minus_x, plus_x, slices=range(NT)):
    lane = lax.broadcasted_iota(jnp.int32, (FACE, EYZ), 1) % EZ
    for s in slices:
        lanes = slice(EYZ * s, EYZ * (s + 1))
        value = state[at, s]
        put(b, 0, lanes, value)
        if minus_x is not None:
            put(b, FP, lanes, minus_x(s))
            put(b, FP + FACE, lanes, plus_x(s))
        put(b, FP + 2 * FACE, lanes, pltpu.roll(y_face(value, 3), EZ, 1))
        put(b, FP + 3 * FACE, lanes, pltpu.roll(y_face(value, 0), EYZ - EZ, 1))
        low_z = state[at, s, pl.ds(3, FACE, stride=4), :]
        high_z = state[at, s, pl.ds(0, FACE, stride=4), :]
        low_z = jnp.where(
            lane == 0, pltpu.roll(low_z, EYZ - EZ + 1, 1), pltpu.roll(low_z, 1, 1)
        )
        high_z = jnp.where(
            lane == EZ - 1, pltpu.roll(high_z, EZ - 1, 1), pltpu.roll(high_z, EYZ - 1, 1)
        )
        put(b, FP + 4 * FACE, lanes, low_z)
        put(b, FP + 5 * FACE, lanes, high_z)


def prepare(own, far, volume, faces, rate, op_r, op_x, op_c, y, part, bc, b):
    step = 0.25
    side_by_side(op_c, *split(step * rate[...]), CMAIN, CREST)
    for k, start in enumerate((own[...], far[0], far[1])):
        y[k, 0] = start
    for n in range(NT - 1):
        for k, value in enumerate(coarse(op_c, bc, [y[k, n] for k in range(3)])):
            y[k, n + 1] = value

    def placed(rows, first):
        at = lax.broadcasted_iota(jnp.int32, (rows, KR), 0) + first
        return jnp.where(at == lax.broadcasted_iota(jnp.int32, (rows, KR), 1), 1.0, 0.0).astype(BF)

    here, there = placed(FP, 0), placed(6 * FACE, FP)
    volumes = split(0.5 * step * volume[...])
    fluxes = split(0.5 * step * faces[...])
    high, low = [
        (dot(v, here) + dot_first(f, there)).astype(BF) for v, f in zip(volumes, fluxes)
    ]
    side_by_side(op_r, high, low, MAIN, REST)
    for k, columns in enumerate((high, low, high)):
        op_x[:, 2 * FACE * k : 2 * FACE * (k + 1)] = columns[:, FP : FP + 2 * FACE]

    gather(b, y, 0, None, None)
    for k in range(3):
        b[MAIN * k + FP : MAIN * k + FP + 2 * FACE] = jnp.zeros((2 * FACE, NT * EYZ), BF)
    product = dot(op_r[...], b[...])
    for s in range(NT):
        part[s] = y[0, s] + lanes_of(product, s)


def sweeps(ready, part, near, op_r, op_x, op_c, starts, ends, y, u1, u2, yp, w, v, b0, b1, b2, b3, bx, bc, bd, up_op, lo_op):
    core, place_here = lax.axis_index("tm"), lax.axis_index("space")
    col, odd_row = lax.rem(place_here, ROW), lax.rem(lax.div(place_here, ROW), 2)

    def place(mate, own_block, other_block):
        y[mate - col + HALO, 0] = own_block
        y[jnp.where(mate > col, mate - col, mate - col + WIN - 1), 0] = other_block

    place(col + 1 - 2 * lax.rem(col, 2), near[0, 0:FP], near[0, FP : 2 * FP])
    place(ROW - 1 - col, near[1, 0:FP], near[1, FP : 2 * FP])
    place(lax.rem(col + 2, ROW), near[0, 2 * FP : 3 * FP], near[1, 2 * FP : 3 * FP])
    for s in range(NT):
        y[HALO, s] = ready[0, s]
        y[2 * HALO, s] = ready[1 + odd_row, s]
        y[0, s] = ready[2 - odd_row, s]

    for f in range(F):
        up_op[16 * f : 16 * f + 16] = op_r[64 * f + 48 : 64 * f + 64]
        lo_op[16 * f : 16 * f + 16] = op_r[64 * f : 64 * f + 16]

    def x_face(state, at, level):
        return lambda s: x_rows(state[at, s], level)

    def x_store(state, at, s, level, rows):
        for f in range(F):
            state[at, s, 64 * f + 16 * level : 64 * f + 16 * level + 16] = rows[
                16 * f : 16 * f + 16
            ]

    here = (1, 2, 3, 5, 6, 7)
    for n in range(NT - 1):
        for k, value in zip(here, coarse(op_c, bc, [y[k, n] for k in here])):
            y[k, n + 1] = value

    def node(target, source, k, level=None, slices=None):
        slices = range(NT) if slices is None else slices
        low, high = EYZ * slices[0], EYZ * (slices[-1] + 1)

        def load(b):
            gather(b, source, k + 1, x_face(source, k, 3), x_face(source, k + 2, 0), slices)

        def run(b):
            if level is None:
                product = dot(op_r[...], b[:, low:high])
            else:
                product = dot((lo_op if level == 0 else up_op)[...], b[:, low:high])
            for j, s in enumerate(slices):
                if level is None:
                    target[k, s] = source[k + 1, s] + lanes_of(product, j)
                else:
                    x_store(
                        target, k, s, level, x_rows(source[k + 1, s], level) + lanes_of(product, j)
                    )

        return load, run

    def first_here():
        def load(b):
            for s in range(NT):
                lanes = slice(EYZ * s, EYZ * (s + 1))
                for j, rows in enumerate((x_rows(y[HALO - 1, s], 3), x_rows(y[HALO + 1, s], 0))):
                    high, low = split(rows)
                    for k, piece in enumerate((high, high, low)):
                        at = 2 * FACE * k + FACE * j
                        bx[at : at + FACE, lanes] = piece

        def run(b):
            product = dot(op_x[...], bx[...])
            for s in range(NT):
                u1[3, s] = part[s] + lanes_of(product, s)

        return load, run

    def first(k):
        return node(u1, y, k, {0: 3, 6: 0}.get(k))

    def second(k, *rest):
        return node(u2, u1, k, *rest)

    tasks = [
        first(0),
        first(1),
        first(2),
        first_here(),
        second(0, None, range(2)),
        second(0, 3, range(2, 4)),
        first(4),
        second(1),
        first(5),
        second(2),
        first(6),
        second(3),
        second(4, None, range(2)),
        second(4, 0, range(2, 4)),
    ]
    buffers = (b0, b1, b2, b3)
    tasks[0][0](b0)
    tasks[1][0](b1)
    for i, (_, run) in enumerate(tasks):
        if i + 2 < len(tasks) and i in (0, 1):
            tasks[i + 2][0](buffers[(i + 2) % 4])
        run(buffers[i % 4])
        if i + 2 < len(tasks) and i not in (0, 1):
            tasks[i + 2][0](buffers[(i + 2) % 4])

    for k in range(5):
        yp[k, 0] = y[k + 2, 0]
        yp[k, 1] = u2[k, 0]
    for n in (1, 2):
        change = coarse(op_c, bd.at[n - 1], [yp[k, n] - y[k + 2, n] for k in range(5)])
        for k in range(5):
            if n == 2 and k in (0, 4):
                level = 3 if k == 0 else 0
                x_store(
                    yp, k, n + 1, level, x_rows(u2[k, n], level) + x_rows(change[k], level)
                )
            else:
                yp[k, n + 1] = u2[k, n] + change[k]

    for k in range(1, 4):
        for s in range(NT):
            w[k, s] = (5.0 / 12.0) * yp[k, s] + (2.0 / 3.0) * u1[k + 1, s] - (1.0 / 12.0) * u2[k, s]
    for k, level in ((0, 3), (4, 0)):
        for s in range(NT):
            x_store(
                w,
                k,
                s,
                level,
                (5.0 / 12.0) * x_rows(yp[k, s], level)
                + (2.0 / 3.0) * x_rows(u1[k + 1, s], level)
                - (1.0 / 12.0) * x_rows(u2[k, s], level),
            )

    def combine(start, one, two, product):
        return (1.0 / 3.0) * (start + one + two) + (start + product)

    def side(at, level, op, b):
        product = dot(op[...], b[...])
        return [
            combine(
                x_rows(yp[at, s], level),
                x_rows(u1[at + 1, s], level),
                x_rows(u2[at, s], level),
                lanes_of(product, s),
            )
            for s in range(NT)
        ]

    gather(b0, w, 2, x_face(w, 1, 3), x_face(w, 3, 0))
    gather(b1, w, 1, x_face(w, 0, 3), x_face(w, 2, 0))
    product = dot(op_r[...], b0[...])
    for s in range(NT):
        v[0, s] = combine(yp[2, s], u1[3, s], u2[2, s], lanes_of(product, s))
    gather(b2, w, 3, x_face(w, 2, 3), x_face(w, 4, 0))
    below = side(1, 3, up_op, b1)
    above = side(3, 0, lo_op, b2)
    gather(b3, v, 0, lambda s: below[s], lambda s: above[s])
    product = dot(op_r[...], b3[...])
    last = [yp[2, s] + lanes_of(product, s) for s in range(NT)]

    begin = [y[HALO, 0], last[0]]
    for n in (1, 2):
        begin.append(last[n] + coarse(op_c, bc, [begin[n] - yp[2, n]])[0])

    @pl.when(core == 0)
    def _():
        for k in range(2):
            starts[k] = begin[k]
            ends[k] = last[k]

    @pl.when(core == 1)
    def _():
        for k in range(2):
            starts[k] = begin[2 + k]
            ends[k] = last[2 + k]


VMEM = pl.BlockSpec(memory_space=pltpu.VMEM)
LIMIT = pltpu.CompilerParams(vmem_limit_bytes=48 << 20)


def ready_made(own, far, volume, faces, rate):
    return pl.pallas_call(
        prepare,
        out_shape=(
            jax.ShapeDtypeStruct((FP, 3 * KR), BF),
            jax.ShapeDtypeStruct((FP, 6 * FACE), BF),
            jax.ShapeDtypeStruct((FP, 3 * FP), BF),
            jax.ShapeDtypeStruct((3, NT, FP, EYZ), F32),
            jax.ShapeDtypeStruct((NT, FP, EYZ), F32),
        ),
        in_specs=[VMEM] * 5,
        out_specs=(VMEM,) * 5,
        scratch_shapes=[
            pltpu.VMEM((3 * FP, 3 * EYZ), BF),
            pltpu.VMEM((3 * KR, NT * EYZ), BF),
        ],
        compiler_params=pltpu.CompilerParams(vmem_limit_bytes=24 << 20),
        cost_estimate=pl.CostEstimate(
            flops=4 * 10**9, bytes_accessed=6 * 10**6, transcendentals=0
        ),
        name="prepare",
    )(own, far, volume, faces, rate)


def work(ready, part, near, op_r, op_x, op_c):
    out = jax.ShapeDtypeStruct((2, FP, EYZ), F32)
    return pl.pallas_call(
        sweeps,
        out_shape=(out, out),
        in_specs=[VMEM] * 6,
        out_specs=(VMEM, VMEM),
        scratch_shapes=[
            pltpu.VMEM((WIN, NT, FP, EYZ), F32),
            pltpu.VMEM((7, NT, FP, EYZ), F32),
            pltpu.VMEM((5, NT, FP, EYZ), F32),
            pltpu.VMEM((5, NT, FP, EYZ), F32),
            pltpu.VMEM((5, NT, FP, EYZ), F32),
            pltpu.VMEM((1, NT, FP, EYZ), F32),
            pltpu.VMEM((3 * KR, NT * EYZ), BF),
            pltpu.VMEM((3 * KR, NT * EYZ), BF),
            pltpu.VMEM((3 * KR, NT * EYZ), BF),
            pltpu.VMEM((3 * KR, NT * EYZ), BF),
            pltpu.VMEM((6 * FACE, NT * EYZ), BF),
            pltpu.VMEM((3 * FP, 6 * EYZ), BF),
            pltpu.VMEM((2, 3 * FP, 5 * EYZ), BF),
            pltpu.VMEM((FACE, 3 * KR), BF),
            pltpu.VMEM((FACE, 3 * KR), BF),
        ],
        compiler_params=LIMIT,
        name="sweeps",
    )(ready, part, near, op_r, op_x, op_c)


def pairs(mate_of, spaces):
    groups = []
    for core in range(2):
        for place in range(spaces):
            mate = mate_of(core, place)
            assert mate_of(core, mate) == place
            if place < mate:
                groups.append([core * spaces + place, core * spaces + mate])
    return groups


def swapped(block, mate_of, spaces):
    both = lax.all_gather(block, ("tm", "space"), axis_index_groups=pairs(mate_of, spaces))
    core, place = lax.axis_index("tm"), lax.axis_index("space")
    first = mate_of(core, place) > place
    return jnp.where(first, both[1], both[0]), jnp.where(first, both[0], both[1])


def sent(block, mate_of, spaces):
    route = [route for a, b in pairs(mate_of, spaces) for route in ((a, b), (b, a))]
    return lax.ppermute(block, ("tm", "space"), route)


def other_row(spaces):
    def mate_of(core, place):
        down = (place // ROW + core) % 2
        return (place + ROW - 2 * ROW * down + spaces) % spaces

    return mate_of


def row_near(core, place):
    base, col = place // ROW * ROW, place % ROW
    return base + (1 - core) * (col + 1 - 2 * (col % 2)) + core * (ROW - 1 - col)


def row_far(core, place):
    return place // ROW * ROW + (place % ROW + 2) % ROW


def per_device(initial_state, volume_block, face_blocks, coarse_rate):
    spaces = lax.axis_size("space")
    core, place = lax.axis_index("tm"), lax.axis_index("space")
    col, odd_row = place % ROW, place // ROW % 2
    own = initial_state[0]

    across, own = swapped(own, other_row(spaces), spaces)
    far = lax.all_gather(across, "tm")
    above, below = far[odd_row], far[1 - odd_row]

    distant = sent(jnp.where(core == 0, own, jnp.where(col < 2, above, below)), row_far, spaces)
    gives_above = jnp.where(core == 0, col % 2 == 0, col < 2)
    close = sent(
        jnp.concatenate([own, jnp.where(gives_above, above, below)], axis=0), row_near, spaces
    )
    faces = jnp.transpose(face_blocks, (0, 2, 1)).reshape(6 * FACE, FP)
    op_r, op_x, op_c, ready, part = ready_made(own, far, volume_block, faces, coarse_rate)
    near = lax.all_gather(jnp.concatenate([close, distant], axis=0), "tm")

    starts, ends = work(ready, part, near, op_r, op_x, op_c)
    return starts[:, None], ends[:, None]


def solution(mesh):
    return jax.shard_map(
        per_device,
        mesh=mesh,
        in_specs=(P("space", None, None), P(), P(), P()),
        out_specs=(P("tm", "space", None, None), P("tm", "space", None, None)),
        check_vma=False,
    )
```

```python
import functools

import jax
import jax.numpy as jnp
from jax import lax
from jax.experimental import pallas as pl
from jax.experimental.pallas import tpu as pltpu
from jax.sharding import PartitionSpec as P

F = 5
EZ = 8
FP = 320
FACE = 80
EYZ = 128
NT = 4
ROW = 4
HALO = 4
WIN = 2 * HALO + 1
KR = FP + 6 * FACE
MAIN = 768
REST = KR - MAIN
CMAIN = 256
CREST = FP - CMAIN
BF = jnp.bfloat16
F32 = jnp.float32


def split(value):
    high = value.astype(BF)
    low = (value - high.astype(F32)).astype(BF)
    return high, low


def dot(left, right):
    return jnp.dot(left, right, preferred_element_type=F32)


def dot_first(left, right):
    return lax.dot_general(left, right, (((0,), (0,)), ((), ())), preferred_element_type=F32)


def x_rows(piece, level):
    return jnp.concatenate(
        [piece[f * 64 + 16 * level : f * 64 + 16 * level + 16] for f in range(F)], axis=0
    )


def y_face(value, level):
    wide = value.reshape(10, 32, EYZ)
    half = 8 * (level // 2)
    first, second = wide[:, half : half + 8], wide[:, 16 + half : 24 + half]
    upper_half = lax.broadcasted_iota(jnp.int32, (10, 8, EYZ), 1) >= 4
    if level % 2 == 1:
        first = pltpu.roll(first, 4, 1)
    else:
        second = pltpu.roll(second, 4, 1)
    return jnp.where(upper_half, second, first).reshape(FACE, EYZ)


def lanes_of(product, s):
    return product[:, EYZ * s : EYZ * (s + 1)]


def side_by_side(ref, high, low, main, rest):
    for k, part in enumerate((high, low, high)):
        ref[:, main * k : main * (k + 1)] = part[:, :main]
        ref[:, 3 * main + rest * k : 3 * main + rest * (k + 1)] = part[:, main:]


def coarse(op_c, bc, values):
    for k, value in enumerate(values):
        lanes = slice(EYZ * k, EYZ * (k + 1))
        high, low = split(value)
        for j, part in enumerate((high, high, low)):
            bc[CMAIN * j : CMAIN * (j + 1), lanes] = part[:CMAIN]
            bc[3 * CMAIN + CREST * j : 3 * CMAIN + CREST * (j + 1), lanes] = part[CMAIN:]
    product = dot(op_c[...], bc[:, : EYZ * len(values)])
    return [value + lanes_of(product, k) for k, value in enumerate(values)]


def put(b, base, lanes, value):
    rows = value.shape[0]
    whole = min(rows, MAIN - base)
    high, low = split(value)
    for k, part in enumerate((high, high, low)):
        b[MAIN * k + base : MAIN * k + base + whole, lanes] = part[:whole]
        if whole < rows:
            b[3 * MAIN + REST * k : 3 * MAIN + REST * (k + 1), lanes] = part[whole:]


def gather(b, state, at, minus_x, plus_x, slices=range(NT)):
    lane = lax.broadcasted_iota(jnp.int32, (FACE, EYZ), 1) % EZ
    for s in slices:
        lanes = slice(EYZ * s, EYZ * (s + 1))
        value = state[at, s]
        put(b, 0, lanes, value)
        if minus_x is not None:
            put(b, FP, lanes, minus_x(s))
            put(b, FP + FACE, lanes, plus_x(s))
        put(b, FP + 2 * FACE, lanes, pltpu.roll(y_face(value, 3), EZ, 1))
        put(b, FP + 3 * FACE, lanes, pltpu.roll(y_face(value, 0), EYZ - EZ, 1))
        low_z = state[at, s, pl.ds(3, FACE, stride=4), :]
        high_z = state[at, s, pl.ds(0, FACE, stride=4), :]
        low_z = jnp.where(
            lane == 0, pltpu.roll(low_z, EYZ - EZ + 1, 1), pltpu.roll(low_z, 1, 1)
        )
        high_z = jnp.where(
            lane == EZ - 1, pltpu.roll(high_z, EZ - 1, 1), pltpu.roll(high_z, EYZ - 1, 1)
        )
        put(b, FP + 4 * FACE, lanes, low_z)
        put(b, FP + 5 * FACE, lanes, high_z)


def prepare(own, far, volume, faces, rate, op_r, op_x, op_c, y, part, bc, b):
    step = 0.25
    side_by_side(op_c, *split(step * rate[...]), CMAIN, CREST)
    for k, start in enumerate((own[...], far[0], far[1])):
        y[k, 0] = start
    for n in range(NT - 1):
        for k, value in enumerate(coarse(op_c, bc, [y[k, n] for k in range(3)])):
            y[k, n + 1] = value

    def placed(rows, first):
        at = lax.broadcasted_iota(jnp.int32, (rows, KR), 0) + first
        return jnp.where(at == lax.broadcasted_iota(jnp.int32, (rows, KR), 1), 1.0, 0.0).astype(BF)

    here, there = placed(FP, 0), placed(6 * FACE, FP)
    volumes = split(0.5 * step * volume[...])
    fluxes = split(0.5 * step * faces[...])
    high, low = [
        (dot(v, here) + dot_first(f, there)).astype(BF) for v, f in zip(volumes, fluxes)
    ]
    side_by_side(op_r, high, low, MAIN, REST)
    for k, columns in enumerate((high, low, high)):
        op_x[:, 2 * FACE * k : 2 * FACE * (k + 1)] = columns[:, FP : FP + 2 * FACE]

    gather(b, y, 0, None, None)
    for k in range(3):
        b[MAIN * k + FP : MAIN * k + FP + 2 * FACE] = jnp.zeros((2 * FACE, NT * EYZ), BF)
    product = dot(op_r[...], b[...])
    for s in range(NT):
        part[s] = y[0, s] + lanes_of(product, s)


def sweeps(ready, part, near, op_r, op_x, op_c, starts, ends, y, u1, u2, yp, w, v, b0, b1, b2, b3, b4, b5, b6, b7, bx, bc, bd, up_op, lo_op):
    core, place_here = lax.axis_index("tm"), lax.axis_index("space")
    col, odd_row = lax.rem(place_here, ROW), lax.rem(lax.div(place_here, ROW), 2)

    def place(mate, own_block, other_block):
        y[mate - col + HALO, 0] = own_block
        y[jnp.where(mate > col, mate - col, mate - col + WIN - 1), 0] = other_block

    place(col + 1 - 2 * lax.rem(col, 2), near[0, 0:FP], near[0, FP : 2 * FP])
    place(ROW - 1 - col, near[1, 0:FP], near[1, FP : 2 * FP])
    place(lax.rem(col + 2, ROW), near[0, 2 * FP : 3 * FP], near[1, 2 * FP : 3 * FP])
    for s in range(NT):
        y[HALO, s] = ready[0, s]
        y[2 * HALO, s] = ready[1 + odd_row, s]
        y[0, s] = ready[2 - odd_row, s]

    for f in range(F):
        up_op[16 * f : 16 * f + 16] = op_r[64 * f + 48 : 64 * f + 64]
        lo_op[16 * f : 16 * f + 16] = op_r[64 * f : 64 * f + 16]

    def x_face(state, at, level):
        return lambda s: x_rows(state[at, s], level)

    def x_store(state, at, s, level, rows):
        for f in range(F):
            state[at, s, 64 * f + 16 * level : 64 * f + 16 * level + 16] = rows[
                16 * f : 16 * f + 16
            ]

    here = (1, 2, 3, 5, 6, 7)
    for n in range(NT - 1):
        for k, value in zip(here, coarse(op_c, bc, [y[k, n] for k in here])):
            y[k, n + 1] = value

    def node(target, source, k, level=None, slices=None):
        slices = range(NT) if slices is None else slices
        low, high = EYZ * slices[0], EYZ * (slices[-1] + 1)

        def load(b):
            gather(b, source, k + 1, x_face(source, k, 3), x_face(source, k + 2, 0), slices)

        def run(b):
            if level is None:
                product = dot(op_r[...], b[:, low:high])
            else:
                product = dot((lo_op if level == 0 else up_op)[...], b[:, low:high])
            for j, s in enumerate(slices):
                if level is None:
                    target[k, s] = source[k + 1, s] + lanes_of(product, j)
                else:
                    x_store(
                        target, k, s, level, x_rows(source[k + 1, s], level) + lanes_of(product, j)
                    )

        return load, run

    def first_here():
        def load(b):
            for s in range(NT):
                lanes = slice(EYZ * s, EYZ * (s + 1))
                for j, rows in enumerate((x_rows(y[HALO - 1, s], 3), x_rows(y[HALO + 1, s], 0))):
                    high, low = split(rows)
                    for k, piece in enumerate((high, high, low)):
                        at = 2 * FACE * k + FACE * j
                        bx[at : at + FACE, lanes] = piece

        def run(b):
            product = dot(op_x[...], bx[...])
            for s in range(NT):
                u1[3, s] = part[s] + lanes_of(product, s)

        return load, run

    def first(k):
        return node(u1, y, k, {0: 3, 6: 0}.get(k))

    def second(k, *rest):
        return node(u2, u1, k, *rest)

    tasks = [
        first(0),
        first(1),
        first(2),
        first_here(),
        second(0, None, range(2)),
        second(0, 3, range(2, 4)),
        first(4),
        second(1),
        first(5),
        second(2),
        first(6),
        second(3),
        second(4, None, range(2)),
        second(4, 0, range(2, 4)),
    ]
    buffers = (b0, b1, b2, b3, b4, b5, b6, b7)
    tasks[0][0](b0)
    tasks[1][0](b1)
    for i, (_, run) in enumerate(tasks):
        if i + 2 < len(tasks) and i in (0, 1):
            tasks[i + 2][0](buffers[(i + 2) % 8])
        run(buffers[i % 8])
        if i + 2 < len(tasks) and i not in (0, 1):
            tasks[i + 2][0](buffers[(i + 2) % 8])

    for k in range(5):
        yp[k, 0] = y[k + 2, 0]
        yp[k, 1] = u2[k, 0]
    for n in (1, 2):
        change = coarse(op_c, bd.at[n - 1], [yp[k, n] - y[k + 2, n] for k in range(5)])
        for k in range(5):
            if n == 2 and k in (0, 4):
                level = 3 if k == 0 else 0
                x_store(
                    yp, k, n + 1, level, x_rows(u2[k, n], level) + x_rows(change[k], level)
                )
            else:
                yp[k, n + 1] = u2[k, n] + change[k]

    for k in range(1, 4):
        for s in range(NT):
            w[k, s] = (5.0 / 12.0) * yp[k, s] + (2.0 / 3.0) * u1[k + 1, s] - (1.0 / 12.0) * u2[k, s]
    for k, level in ((0, 3), (4, 0)):
        for s in range(NT):
            x_store(
                w,
                k,
                s,
                level,
                (5.0 / 12.0) * x_rows(yp[k, s], level)
                + (2.0 / 3.0) * x_rows(u1[k + 1, s], level)
                - (1.0 / 12.0) * x_rows(u2[k, s], level),
            )

    def combine(start, one, two, product):
        return (1.0 / 3.0) * (start + one + two) + (start + product)

    def side(at, level, op, b):
        product = dot(op[...], b[...])
        return [
            combine(
                x_rows(yp[at, s], level),
                x_rows(u1[at + 1, s], level),
                x_rows(u2[at, s], level),
                lanes_of(product, s),
            )
            for s in range(NT)
        ]

    gather(b0, w, 2, x_face(w, 1, 3), x_face(w, 3, 0))
    gather(b1, w, 1, x_face(w, 0, 3), x_face(w, 2, 0))
    product = dot(op_r[...], b0[...])
    for s in range(NT):
        v[0, s] = combine(yp[2, s], u1[3, s], u2[2, s], lanes_of(product, s))
    gather(b2, w, 3, x_face(w, 2, 3), x_face(w, 4, 0))
    below = side(1, 3, up_op, b1)
    above = side(3, 0, lo_op, b2)
    gather(b3, v, 0, lambda s: below[s], lambda s: above[s])
    product = dot(op_r[...], b3[...])
    last = [yp[2, s] + lanes_of(product, s) for s in range(NT)]

    begin = [y[HALO, 0], last[0]]
    for n in (1, 2):
        begin.append(last[n] + coarse(op_c, bc, [begin[n] - yp[2, n]])[0])

    @pl.when(core == 0)
    def _():
        for k in range(2):
            starts[k] = begin[k]
            ends[k] = last[k]

    @pl.when(core == 1)
    def _():
        for k in range(2):
            starts[k] = begin[2 + k]
            ends[k] = last[2 + k]


VMEM = pl.BlockSpec(memory_space=pltpu.VMEM)
LIMIT = pltpu.CompilerParams(vmem_limit_bytes=48 << 20)


def ready_made(own, far, volume, faces, rate):
    return pl.pallas_call(
        prepare,
        out_shape=(
            jax.ShapeDtypeStruct((FP, 3 * KR), BF),
            jax.ShapeDtypeStruct((FP, 6 * FACE), BF),
            jax.ShapeDtypeStruct((FP, 3 * FP), BF),
            jax.ShapeDtypeStruct((3, NT, FP, EYZ), F32),
            jax.ShapeDtypeStruct((NT, FP, EYZ), F32),
        ),
        in_specs=[VMEM] * 5,
        out_specs=(VMEM,) * 5,
        scratch_shapes=[
            pltpu.VMEM((3 * FP, 3 * EYZ), BF),
            pltpu.VMEM((3 * KR, NT * EYZ), BF),
        ],
        compiler_params=pltpu.CompilerParams(vmem_limit_bytes=24 << 20),
        cost_estimate=pl.CostEstimate(
            flops=4 * 10**9, bytes_accessed=6 * 10**6, transcendentals=0
        ),
        name="prepare",
    )(own, far, volume, faces, rate)


def work(ready, part, near, op_r, op_x, op_c):
    out = jax.ShapeDtypeStruct((2, FP, EYZ), F32)
    return pl.pallas_call(
        sweeps,
        out_shape=(out, out),
        in_specs=[VMEM] * 6,
        out_specs=(VMEM, VMEM),
        scratch_shapes=[
            pltpu.VMEM((WIN, NT, FP, EYZ), F32),
            pltpu.VMEM((7, NT, FP, EYZ), F32),
            pltpu.VMEM((5, NT, FP, EYZ), F32),
            pltpu.VMEM((5, NT, FP, EYZ), F32),
            pltpu.VMEM((5, NT, FP, EYZ), F32),
            pltpu.VMEM((1, NT, FP, EYZ), F32),
            pltpu.VMEM((3 * KR, NT * EYZ), BF),
            pltpu.VMEM((3 * KR, NT * EYZ), BF),
            pltpu.VMEM((3 * KR, NT * EYZ), BF),
            pltpu.VMEM((3 * KR, NT * EYZ), BF),
            pltpu.VMEM((3 * KR, NT * EYZ), BF),
            pltpu.VMEM((3 * KR, NT * EYZ), BF),
            pltpu.VMEM((3 * KR, NT * EYZ), BF),
            pltpu.VMEM((3 * KR, NT * EYZ), BF),
            pltpu.VMEM((6 * FACE, NT * EYZ), BF),
            pltpu.VMEM((3 * FP, 6 * EYZ), BF),
            pltpu.VMEM((2, 3 * FP, 5 * EYZ), BF),
            pltpu.VMEM((FACE, 3 * KR), BF),
            pltpu.VMEM((FACE, 3 * KR), BF),
        ],
        compiler_params=LIMIT,
        name="sweeps",
    )(ready, part, near, op_r, op_x, op_c)


def pairs(mate_of, spaces):
    groups = []
    for core in range(2):
        for place in range(spaces):
            mate = mate_of(core, place)
            assert mate_of(core, mate) == place
            if place < mate:
                groups.append([core * spaces + place, core * spaces + mate])
    return groups


def swapped(block, mate_of, spaces):
    both = lax.all_gather(block, ("tm", "space"), axis_index_groups=pairs(mate_of, spaces))
    core, place = lax.axis_index("tm"), lax.axis_index("space")
    first = mate_of(core, place) > place
    return jnp.where(first, both[1], both[0]), jnp.where(first, both[0], both[1])


def sent(block, mate_of, spaces):
    route = [route for a, b in pairs(mate_of, spaces) for route in ((a, b), (b, a))]
    return lax.ppermute(block, ("tm", "space"), route)


def other_row(spaces):
    def mate_of(core, place):
        down = (place // ROW + core) % 2
        return (place + ROW - 2 * ROW * down + spaces) % spaces

    return mate_of


def row_near(core, place):
    base, col = place // ROW * ROW, place % ROW
    return base + (1 - core) * (col + 1 - 2 * (col % 2)) + core * (ROW - 1 - col)


def row_far(core, place):
    return place // ROW * ROW + (place % ROW + 2) % ROW


def per_device(initial_state, volume_block, face_blocks, coarse_rate):
    spaces = lax.axis_size("space")
    core, place = lax.axis_index("tm"), lax.axis_index("space")
    col, odd_row = place % ROW, place // ROW % 2
    own = initial_state[0]

    across, own = swapped(own, other_row(spaces), spaces)
    far = lax.all_gather(across, "tm")
    above, below = far[odd_row], far[1 - odd_row]

    distant = sent(jnp.where(core == 0, own, jnp.where(col < 2, above, below)), row_far, spaces)
    gives_above = jnp.where(core == 0, col % 2 == 0, col < 2)
    close = sent(
        jnp.concatenate([own, jnp.where(gives_above, above, below)], axis=0), row_near, spaces
    )
    faces = jnp.transpose(face_blocks, (0, 2, 1)).reshape(6 * FACE, FP)
    op_r, op_x, op_c, ready, part = ready_made(own, far, volume_block, faces, coarse_rate)
    near = lax.all_gather(jnp.concatenate([close, distant], axis=0), "tm")

    starts, ends = work(ready, part, near, op_r, op_x, op_c)
    return starts[:, None], ends[:, None]


def solution(mesh):
    return jax.shard_map(
        per_device,
        mesh=mesh,
        in_specs=(P("space", None, None), P(), P(), P()),
        out_specs=(P("tm", "space", None, None), P("tm", "space", None, None)),
        check_vma=False,
    )
```
